32 devices in a mesh: group: 2 (over x), seq: 16 (over z, y, core).
Axes of the slice: x: 2, y: 2, z: 4, core: 2. Of those that a mesh axis runs over, the one named last changes fastest.
Arguments:
- queries: bfloat16 [4, 2048, 4096], P('group', 'seq'), parts along dimension 0, may hold values from -32 to 32
- key_vectors: bfloat16 [4, 2048, 4096], P('group', 'seq'), parts along dimension 0, may hold values from -24 to 24
- value_vectors: bfloat16 [4, 2048, 4096], P('group', 'seq'), parts along dimension 0, may hold values from -6 to 6
- out_grad: bfloat16 [4, 2048, 4096], P('group', 'seq'), parts along dimension 0, may hold values from -6 to 6
Outputs:
- grad_queries: bfloat16 [4, 2048, 4096], P('group', 'seq'), parts along dimension 0
- grad_keys: bfloat16 [4, 2048, 4096], P('group', 'seq'), parts along dimension 0
- grad_values: bfloat16 [4, 2048, 4096], P('group', 'seq'), parts along dimension 0
The draws below stay inside these ranges and needn't reach their ends.
There are 2 independent parts, one for each index of `group`. The reference program is written for one: setup_inputs(seed, part) draws one part's arguments, and reference() takes and returns one part's arrays. A program takes and returns all parts, laid end to end along the dimension named above; each array names one. Nothing has to cross between parts.
All inputs are finite; a program needn't handle non-finite values.
Results may differ from the reference program's by a relative error of at most 0.0052.
Values may be sent and summed in bfloat16 or wider, within the bound.
A program may use at most 128 MiB of HBM per device.

```python
import jax
import jax.numpy as jnp
from jax import lax

HEADS = 32
HEAD_DIM = 128
PAGES = 2
TOKENS = 2048


def draw_pair(key):
    base_key = jax.random.fold_in(key, 4099)
    key_query, key_keys = jax.random.split(base_key, 2)
    feature_width = HEADS * HEAD_DIM
    queries = jnp.clip(jax.random.normal(key_query, (PAGES, TOKENS, feature_width), jnp.float32), -6.0, 6.0)
    key_vectors = jnp.clip(jax.random.normal(key_keys, (PAGES, TOKENS, feature_width), jnp.float32), -6.0, 6.0)
    return (queries, key_vectors)


def draw_queries(key, part):
    return draw_pair(key)[0].astype(jnp.bfloat16)


def draw_key_vectors(key, part):
    return draw_pair(key)[1].astype(jnp.bfloat16)


def steps_of(stream_key, dims, cuts, low, high):
    def one(position, parts):
        heights = jax.random.uniform(jax.random.fold_in(jax.random.fold_in(stream_key, 6), position), (parts,), jnp.float32, low / len(cuts), high / len(cuts))
        return jnp.repeat(jnp.exp(heights), dims[position] // parts).reshape((-1,) + (1,) * (len(dims) - position - 1))

    gain = one(*cuts[0])
    for cut in cuts[1:]:
        gain = gain * one(*cut)
    return gain


def gaussian(key, extent, deviation, reach, cuts=(), kind=jnp.bfloat16):
    entries = deviation * jax.random.normal(key, extent, jnp.float32)
    if cuts:
        entries = entries * steps_of(key, extent, cuts, -0.22, 0.18)
    return jnp.clip(entries, -reach, reach).astype(kind)


def setup_inputs(seed: int = 0, part: int = 0) -> dict:
    splits = jax.random.split(jax.random.key(seed), 5)
    own_keys = jax.random.split(jax.random.fold_in(splits[4], part), 5)
    queries = draw_queries(jax.random.fold_in(jax.random.fold_in(splits[4], part), 71), part)
    key_vectors = draw_key_vectors(jax.random.fold_in(jax.random.fold_in(splits[4], part), 71), part)
    value_vectors = gaussian(own_keys[2], (PAGES, TOKENS, HEADS * HEAD_DIM), 1.0, 6.0, ((1, 16),))
    out_grad = gaussian(own_keys[3], (PAGES, TOKENS, HEADS * HEAD_DIM), 1.0, 6.0, ((1, 16),))
    return {"queries": queries, "key_vectors": key_vectors, "value_vectors": value_vectors, "out_grad": out_grad}


def single_head(operands):
    queries, key_vectors, value_vectors, out_grad = operands
    tokens_all = queries.shape[0]
    score_scale = queries.shape[1] ** -0.5
    scores = jnp.dot(queries, key_vectors.T, preferred_element_type=jnp.float32) * score_scale
    positions = jnp.arange(tokens_all, dtype=jnp.int32)
    causal_mask = positions[:, None] >= positions[None, :]
    scores = jnp.where(causal_mask, scores, -jnp.inf)
    row_top = jnp.max(scores, axis=1, keepdims=True)
    weights = jnp.exp(scores - row_top)
    softmax_rows = weights / jnp.sum(weights, axis=1, keepdims=True)
    probs_low = softmax_rows.astype(jnp.bfloat16)
    dprobs = jnp.dot(out_grad, value_vectors.T, preferred_element_type=jnp.float32)
    row_delta = jnp.sum(softmax_rows * dprobs, axis=1, keepdims=True)
    dscores = (softmax_rows * (dprobs - row_delta)).astype(jnp.bfloat16)
    grad_values = jnp.dot(probs_low.T, out_grad, preferred_element_type=jnp.float32).astype(jnp.bfloat16)
    grad_queries = (jnp.dot(dscores, key_vectors, preferred_element_type=jnp.float32) * score_scale).astype(jnp.bfloat16)
    grad_keys = (jnp.dot(dscores.T, queries, preferred_element_type=jnp.float32) * score_scale).astype(jnp.bfloat16)
    return grad_queries, grad_keys, grad_values


def to_heads(operand):
    shaped = operand.reshape(PAGES, TOKENS, HEADS, HEAD_DIM).transpose(0, 2, 1, 3)
    return shaped.reshape(PAGES * HEADS, TOKENS, HEAD_DIM)


def to_tokens(operand):
    shaped = operand.reshape(PAGES, HEADS, TOKENS, HEAD_DIM).transpose(0, 2, 1, 3)
    return shaped.reshape(PAGES, TOKENS, HEADS * HEAD_DIM)


def reference(queries, key_vectors, value_vectors, out_grad):
    gradients = lax.map(single_head, (to_heads(queries), to_heads(key_vectors), to_heads(value_vectors), to_heads(out_grad)))
    return (to_tokens(gradients[0]), to_tokens(gradients[1]), to_tokens(gradients[2]))
```

```python
import functools

import jax
import jax.numpy as jnp
from jax import lax
from jax.experimental import pallas as pl
from jax.experimental.pallas import tpu as pltpu
from jax.sharding import PartitionSpec as P

HEADS = 32
LOG2_E = 1.4426950408889634


def product(a, b, dims):
    return lax.dot_general(a, b, ((dims[:1], dims[1:]), ((), ())), preferred_element_type=jnp.float32)


def gradient_kernel(in_ref, out_ref, score_buf, dprob_buf, key_sum, value_sum):
    sources, _, rows, width = in_ref.shape
    side = score_buf.shape[1]
    per = side // rows
    blocks = sources // per
    scale = width ** (-0.5)

    def block(which, index):
        return in_ref[pl.ds(index * per, per), which].reshape(side, width)

    key_sum[...] = jnp.zeros_like(key_sum)
    value_sum[...] = jnp.zeros_like(value_sum)

    def row_block(i, carry):
        query = block(0, i)
        grad = block(3, i)

        def scan_keys(j, state, diagonal):
            top, total, dot_total = state
            scores = product(block(1, j), query, (1, 1)) * (scale * LOG2_E)
            if diagonal:
                key_ids = lax.broadcasted_iota(jnp.int32, (side, side), 0)
                query_ids = lax.broadcasted_iota(jnp.int32, (side, side), 1)
                scores = jnp.where(query_ids >= key_ids, scores, -jnp.inf)
            dprobs = product(block(2, j), grad, (1, 1))
            score_buf[j] = scores
            dprob_buf[j] = dprobs
            new_top = jnp.maximum(top, jnp.max(scores, axis=0, keepdims=True))
            weights = jnp.exp2(scores - new_top)
            shrink = jnp.exp2(top - new_top)
            total = total * shrink + jnp.sum(weights, axis=0, keepdims=True)
            dot_total = dot_total * shrink + jnp.sum(weights * dprobs, axis=0, keepdims=True)
            return new_top, total, dot_total

        state = (
            jnp.full((1, side), -jnp.inf, jnp.float32),
            jnp.zeros((1, side), jnp.float32),
            jnp.zeros((1, side), jnp.float32),
        )
        state = lax.fori_loop(0, i, functools.partial(scan_keys, diagonal=False), state)
        top, total, dot_total = scan_keys(i, state, True)
        inverse = 1.0 / total
        row_delta = dot_total * inverse

        def add_terms(j, query_sum):
            probs = jnp.exp2(score_buf[j] - top) * inverse
            dscores = (probs * (dprob_buf[j] - row_delta)).astype(jnp.bfloat16)
            span = pl.ds(pl.multiple_of(j * side, side), side)
            value_sum[span] += product(probs.astype(jnp.bfloat16), grad, (1, 0))
            key_sum[span] += product(dscores, query, (1, 0))
            return query_sum + product(dscores, block(1, j), (0, 0))

        query_sum = lax.fori_loop(0, i + 1, add_terms, jnp.zeros((side, width), jnp.float32))
        out_ref[pl.ds(i * per, per), 0] = (
            (query_sum * scale).astype(jnp.bfloat16).reshape(per, rows, width)
        )
        return carry

    lax.fori_loop(0, blocks, row_block, 0)
    out_ref[:, 1] = (key_sum[...] * scale).astype(jnp.bfloat16).reshape(sources, rows, width)
    out_ref[:, 2] = value_sum[...].astype(jnp.bfloat16).reshape(sources, rows, width)


def page_gradients(arrived, head_width):
    sources, _, rows, features = arrived.shape
    tokens = sources * rows
    side = min(512, tokens)
    heads = features // head_width
    return pl.pallas_call(
        gradient_kernel,
        grid=(heads,),
        in_specs=[pl.BlockSpec((sources, 4, rows, head_width), lambda h: (0, 0, 0, h))],
        out_specs=pl.BlockSpec((sources, 3, rows, head_width), lambda h: (0, 0, 0, h)),
        out_shape=jax.ShapeDtypeStruct((sources, 3, rows, features), jnp.bfloat16),
        scratch_shapes=[
            pltpu.VMEM((tokens // side, side, side), jnp.float32),
            pltpu.VMEM((tokens // side, side, side), jnp.float32),
            pltpu.VMEM((tokens, head_width), jnp.float32),
            pltpu.VMEM((tokens, head_width), jnp.float32),
        ],
        compiler_params=pltpu.CompilerParams(vmem_limit_bytes=56 * 1024 * 1024),
        cost_estimate=pl.CostEstimate(
            flops=heads * 5 * tokens * tokens * head_width * 2,
            bytes_accessed=7 * tokens * features * 2,
            transcendentals=heads * tokens * tokens,
        ),
    )(arrived)


def body(devices, queries, key_vectors, value_vectors, out_grad):
    page_count, rows, feature_width = queries.shape
    head_width = feature_width // HEADS
    part = feature_width // devices
    operands = (queries, key_vectors, value_vectors, out_grad)

    def swap(block):
        return lax.all_to_all(block, "seq", split_axis=0, concat_axis=0, tiled=True)

    pages = []
    for page in range(page_count):
        outgoing = jnp.stack([a[page].reshape(rows, devices, part) for a in operands])
        arrived = swap(jnp.transpose(outgoing, (2, 0, 1, 3)))
        returned = swap(page_gradients(arrived, head_width))
        pages.append(jnp.transpose(returned, (1, 2, 0, 3)).reshape(3, rows, feature_width))
    return tuple(jnp.stack([page[k] for page in pages]) for k in range(3))


def solution(mesh):
    placed = P("group", "seq", None)
    return jax.shard_map(
        functools.partial(body, mesh.shape["seq"]),
        mesh=mesh,
        in_specs=(placed,) * 4,
        out_specs=(placed,) * 3,
        check_vma=False,
    )
```

```python
import functools

import jax
import jax.numpy as jnp
from jax import lax
from jax.experimental import pallas as pl
from jax.experimental.pallas import tpu as pltpu
from jax.sharding import PartitionSpec as P

HEADS = 32
LOG2_E = 1.4426950408889634


def product(a, b, dims):
    return lax.dot_general(a, b, ((dims[:1], dims[1:]), ((), ())), preferred_element_type=jnp.float32)


def gradient_kernel(later_ref, kv_ref, qg_ref, prefix_ref, dq_ref, dkv_ref, dprefix_ref, score_buf, dprob_buf, key_sum, value_sum):
    sources, _, rows, width = kv_ref.shape
    side = score_buf.shape[1]
    per = side // rows
    blocks = sources // per
    scale = width ** (-0.5)
    skipped = (1 - later_ref[0]) * blocks

    def block(ref, which, index):
        return ref[pl.ds(index * per, per), which].reshape(side, width)

    key_sum[...] = jnp.zeros_like(key_sum)
    value_sum[...] = jnp.zeros_like(value_sum)

    def row_block(i, carry):
        query = block(qg_ref, 0, i)
        grad = block(qg_ref, 1, i)

        def scan_keys(j, state, source, offset, diagonal):
            top, total, dot_total = state
            scores = product(block(source, 0, j), query, (1, 1)) * (scale * LOG2_E)
            if diagonal:
                key_ids = lax.broadcasted_iota(jnp.int32, (side, side), 0)
                query_ids = lax.broadcasted_iota(jnp.int32, (side, side), 1)
                scores = jnp.where(query_ids >= key_ids, scores, -jnp.inf)
            dprobs = product(block(source, 1, j), grad, (1, 1))
            score_buf[offset + j] = scores
            dprob_buf[offset + j] = dprobs
            new_top = jnp.maximum(top, jnp.max(scores, axis=0, keepdims=True))
            weights = jnp.exp2(scores - new_top)
            shrink = jnp.exp2(top - new_top)
            total = total * shrink + jnp.sum(weights, axis=0, keepdims=True)
            dot_total = dot_total * shrink + jnp.sum(weights * dprobs, axis=0, keepdims=True)
            return new_top, total, dot_total

        state = (
            jnp.full((1, side), -jnp.inf, jnp.float32),
            jnp.zeros((1, side), jnp.float32),
            jnp.zeros((1, side), jnp.float32),
        )
        own = functools.partial(scan_keys, source=kv_ref, offset=blocks)
        earlier = functools.partial(scan_keys, source=prefix_ref, offset=0, diagonal=False)
        state = own(i, state, diagonal=True)
        state = lax.fori_loop(0, i, functools.partial(own, diagonal=False), state)
        top, total, dot_total = lax.fori_loop(skipped, blocks, earlier, state)
        inverse = 1.0 / total
        row_delta = dot_total * inverse

        def add_terms(j, query_sum, source, offset):
            slot = offset + j
            probs = jnp.exp2(score_buf[slot] - top) * inverse
            dscores = (probs * (dprob_buf[slot] - row_delta)).astype(jnp.bfloat16)
            span = pl.ds(pl.multiple_of(slot * side, side), side)
            value_sum[span] += product(probs.astype(jnp.bfloat16), grad, (1, 0))
            key_sum[span] += product(dscores, query, (1, 0))
            return query_sum + product(dscores, block(source, 0, j), (0, 0))

        query_sum = jnp.zeros((side, width), jnp.float32)
        query_sum = lax.fori_loop(
            0, i + 1, functools.partial(add_terms, source=kv_ref, offset=blocks), query_sum
        )
        query_sum = lax.fori_loop(
            skipped, blocks, functools.partial(add_terms, source=prefix_ref, offset=0), query_sum
        )
        dq_ref[pl.ds(i * per, per), 0] = (
            (query_sum * scale).astype(jnp.bfloat16).reshape(per, rows, width)
        )
        return carry

    lax.fori_loop(0, blocks, row_block, 0)
    half = sources * rows
    for start, ref in ((0, dprefix_ref), (half, dkv_ref)):
        span = pl.ds(start, half)
        ref[:, 0] = (key_sum[span] * scale).astype(jnp.bfloat16).reshape(sources, rows, width)
        ref[:, 1] = value_sum[span].astype(jnp.bfloat16).reshape(sources, rows, width)


def page_gradients(later, kv, qg, prefix, head_width):
    sources, _, rows, features = kv.shape
    half = sources * rows
    side = min(512, half)
    heads = features // head_width

    def spec(kinds):
        return pl.BlockSpec((sources, kinds, rows, head_width), lambda h: (0, 0, 0, h))

    def shape(kinds):
        return jax.ShapeDtypeStruct((sources, kinds, rows, features), jnp.bfloat16)

    return pl.pallas_call(
        gradient_kernel,
        grid=(heads,),
        in_specs=[pl.BlockSpec(memory_space=pltpu.SMEM), spec(2), spec(2), spec(2)],
        out_specs=[spec(1), spec(2), spec(2)],
        out_shape=[shape(1), shape(2), shape(2)],
        scratch_shapes=[
            pltpu.VMEM((2 * half // side, side, side), jnp.float32),
            pltpu.VMEM((2 * half // side, side, side), jnp.float32),
            pltpu.VMEM((2 * half, head_width), jnp.float32),
            pltpu.VMEM((2 * half, head_width), jnp.float32),
        ],
        compiler_params=pltpu.CompilerParams(vmem_limit_bytes=56 * 1024 * 1024),
        cost_estimate=pl.CostEstimate(
            flops=heads * 15 * half * half * head_width * 2,
            bytes_accessed=11 * half * features * 2,
            transcendentals=heads * 3 * half * half,
        ),
    )(later, kv, qg, prefix)


def pack_kernel(first_ref, second_ref, out_ref):
    out_ref[0, 0] = first_ref[0]
    out_ref[0, 1] = second_ref[0]


def pack(page, owners, first, second):
    rows, width = first.shape[1:]
    part = width // owners
    source = pl.BlockSpec((1, rows, part), lambda o: (page, 0, o))
    return pl.pallas_call(
        pack_kernel,
        grid=(owners,),
        in_specs=[source, source],
        out_specs=pl.BlockSpec((1, 2, rows, part), lambda o: (o, 0, 0, 0)),
        out_shape=jax.ShapeDtypeStruct((owners, 2, rows, part), jnp.bfloat16),
        cost_estimate=pl.CostEstimate(flops=0, bytes_accessed=8 * rows * width, transcendentals=0),
    )(first, second)


def unpack_kernel(page_count, *refs):
    query_refs, kv_refs = refs[:page_count], refs[page_count : 2 * page_count]
    dq_ref, dk_ref, dv_ref = refs[2 * page_count :]
    for page in range(page_count):
        dq_ref[page] = query_refs[page][0, 0]
        dk_ref[page] = kv_refs[page][0, 0]
        dv_ref[page] = kv_refs[page][0, 1]


def unpack(query_parts, kv_parts):
    page_count = len(query_parts)
    owners, _, rows, part = query_parts[0].shape
    spec = lambda kinds: pl.BlockSpec((1, kinds, rows, part), lambda o: (o, 0, 0, 0))
    result = jax.ShapeDtypeStruct((page_count, rows, owners * part), jnp.bfloat16)
    return pl.pallas_call(
        functools.partial(unpack_kernel, page_count),
        grid=(owners,),
        in_specs=[spec(1)] * page_count + [spec(2)] * page_count,
        out_specs=[pl.BlockSpec((page_count, rows, part), lambda o: (0, 0, o))] * 3,
        out_shape=[result] * 3,
    )(*query_parts, *kv_parts)


def body(devices, queries, key_vectors, value_vectors, out_grad):
    page_count, rows, feature_width = queries.shape
    head_width = feature_width // HEADS
    owners = devices // 2
    halves = [list(range(owners)), list(range(owners, devices))]
    upward = [(i, i + owners) for i in range(owners)]
    downward = [(i + owners, i) for i in range(owners)]
    later = (lax.axis_index("seq") // owners).astype(jnp.int32).reshape(1)

    def swap(block):
        return lax.all_to_all(
            block, "seq", split_axis=0, concat_axis=0, axis_index_groups=halves, tiled=True
        )

    query_parts, kv_parts = [], []
    for page in range(page_count):
        kv = swap(pack(page, owners, key_vectors, value_vectors))
        prefix = lax.ppermute(kv, "seq", upward)
        qg = swap(pack(page, owners, queries, out_grad))
        dq, dkv, dprefix = page_gradients(later, kv, qg, prefix, head_width)
        back = lax.ppermute(dprefix, "seq", downward)
        query_parts.append(swap(dq))
        total = dkv.astype(jnp.float32) + back.astype(jnp.float32)
        kv_parts.append(swap(total.astype(jnp.bfloat16)))
    return tuple(unpack(query_parts, kv_parts))


def solution(mesh):
    placed = P("group", "seq", None)
    return jax.shard_map(
        functools.partial(body, mesh.shape["seq"]),
        mesh=mesh,
        in_specs=(placed,) * 4,
        out_specs=(placed,) * 3,
        check_vma=False,
    )
```
